32 devices in a mesh: dp: 8 (over z, y), shard: 4 (over x, core).
Axes of the slice: x: 2, y: 2, z: 4, core: 2. Of those that a mesh axis runs over, the one named last changes fastest.
Arguments:
- tokens: bfloat16 [32768, 640], P(('dp', 'shard')), may hold values from -6 to 6
- cotangent: bfloat16 [32768, 640], P(('dp', 'shard')), may hold values from -6 to 6
- segment_ids: int32 [32768], P(('dp', 'shard')), may hold values from -1 to 3, as said below
- in_weight: float32 [640, 1536], P('shard'), may hold values from -0.25 to 0.25
- out_weight: float32 [1024, 640], P('shard'), may hold values from -0.1875 to 0.1875
- gate_weight: float32 [640, 4096], P('shard'), may hold values from -0.25 to 0.25
- down_weight: float32 [2048, 640], P('shard'), may hold values from -0.125 to 0.125
- norm_gains: float32 [3072], P('shard'), may hold values from -0.5 to 0.5
- in_first: float32 [640, 1536], P('shard'), may hold values from -112 to 112
- out_first: float32 [1024, 640], P('shard'), may hold values from -112 to 112
- gate_first: float32 [640, 4096], P('shard'), may hold values from -112 to 112
- down_first: float32 [2048, 640], P('shard'), may hold values from -112 to 112
- gain_first: float32 [3072], P('shard'), may hold values from -112 to 112
- in_second: float32 [640, 1536], P('shard'), may hold values from 983.04 to 9830.4
- out_second: float32 [1024, 640], P('shard'), may hold values from 983.04 to 9830.4
- gate_second: float32 [640, 4096], P('shard'), may hold values from 983.04 to 9830.4
- down_second: float32 [2048, 640], P('shard'), may hold values from 983.04 to 9830.4
- gain_second: float32 [3072], P('shard'), may hold values from 983.04 to 9830.4
Outputs:
- layer_out: bfloat16 [32768, 640], P(('dp', 'shard'))
- grad_input: bfloat16 [32768, 640], P(('dp', 'shard'))
- new_in: float32 [640, 1536], P('shard')
- new_out: float32 [1024, 640], P('shard')
- new_gate: float32 [640, 4096], P('shard')
- new_down: float32 [2048, 640], P('shard')
- new_gains: float32 [3072], P('shard')
- in_momentum: float32 [640, 1536], P('shard')
- out_momentum: float32 [1024, 640], P('shard')
- gate_momentum: float32 [640, 4096], P('shard')
- down_momentum: float32 [2048, 640], P('shard')
- gain_momentum: float32 [3072], P('shard')
- in_variance: float32 [640, 1536], P('shard')
- out_variance: float32 [1024, 640], P('shard')
- gate_variance: float32 [640, 4096], P('shard')
- down_variance: float32 [2048, 640], P('shard')
- gain_variance: float32 [3072], P('shard')
The draws below stay inside these ranges and needn't reach their ends.
Inputs may be any that keep to these rules, and one draw needn't show every extreme that they name: `segment_ids`: in each group of 1024 slots the live slots come first, at least 512 of them, holding sequences numbered 0, 1, 2, ... in order (never falling, each at least one slot); the remaining slots are padding, numbered -1. One group holds a single sequence filling all 1024 slots, some group has exactly 512 live slots, and every other group holds 4 sequences.
All inputs are finite; a program needn't handle non-finite values.
Results may differ from the reference program's by a relative error of at most 0.018.
Values may be sent and summed in bfloat16 or wider, within the bound.
A program may use at most 192 MiB of HBM per device.

```python
import math
import jax
import jax.numpy as jnp
from jax import lax

D = 640
HEADS = 4
HEAD = 256
FF = 2048
TOK_DEV = 1024
SEGS = 4
STEP = 10
MIN_LEN = 512
TOKENS = 32768


def draw_segment_ids(key, part):
    key = jax.random.fold_in(key, 7)
    key_len, key_perm, key_cut = jax.random.split(key, 3)
    groups = TOKENS // TOK_DEV
    live_count = jax.random.randint(key_len, (groups,), MIN_LEN, TOK_DEV + 1)
    order = jax.random.permutation(key_perm, groups)
    live_count = live_count.at[order[0]].set(TOK_DEV)
    live_count = live_count.at[order[1]].set(MIN_LEN)
    spacing = MIN_LEN // SEGS
    offsets = jax.random.randint(key_cut, (groups, SEGS - 1), 0, spacing)
    bounds = (jnp.arange(1, SEGS, dtype=jnp.int32) * spacing)[None, :] + offsets
    bounds = bounds.at[order[0]].set(TOK_DEV)
    places = jnp.arange(TOK_DEV, dtype=jnp.int32)
    numbers = jnp.sum((places[None, :, None] >= bounds[:, None, :]).astype(jnp.int32), -1)
    numbers = jnp.where(places[None, :] < live_count[:, None], numbers, -1)
    return numbers.reshape(TOKENS).astype(jnp.int32)


def block_scale(stream_key, extent, pieces, low, top_value):
    def one(axis_at, shards_of):
        draws = jax.random.uniform(jax.random.fold_in(jax.random.fold_in(stream_key, 6), axis_at), (shards_of,), jnp.float32, low / len(pieces), top_value / len(pieces))
        return jnp.repeat(jnp.exp(draws), extent[axis_at] // shards_of).reshape((-1,) + (1,) * (len(extent) - axis_at - 1))

    gain = one(*pieces[0])
    for cut in pieces[1:]:
        gain = gain * one(*cut)
    return gain


def gaussian(key, dims, spread, limit, shards=(), kind=jnp.bfloat16):
    loudness = block_scale(key, dims, shards, -0.22, 0.18) if shards else 1.0
    values = jax.random.normal(key, dims, jnp.float32) * spread * loudness
    return jnp.minimum(jnp.maximum(values, -limit), limit).astype(kind)


def setup_inputs(seed: int = 0) -> dict:
    seeds = jax.random.split(jax.random.key(seed), 19)
    tokens = gaussian(seeds[0], (TOKENS, D), 1.0, 6.0, ((0, 32),))
    cotangent = gaussian(seeds[1], (TOKENS, D), 1.0, 6.0, ((0, 32),))
    segment_ids = draw_segment_ids(jax.random.fold_in(seeds[18], 71), 0)
    in_weight = gaussian(seeds[3], (D, HEADS * HEAD + 2 * HEAD), D ** -0.5, 0.25, ((0, 4),), jnp.float32)
    out_weight = gaussian(seeds[4], (HEADS * HEAD, D), (HEADS * HEAD) ** -0.5, 0.1875, ((0, 4),), jnp.float32)
    gate_weight = gaussian(seeds[5], (D, 2 * FF), D ** -0.5, 0.25, ((0, 4),), jnp.float32)
    down_weight = gaussian(seeds[6], (FF, D), FF ** -0.5, 0.125, ((0, 4),), jnp.float32)
    norm_gains = jnp.clip(jax.random.uniform(seeds[7], (4 * D + 2 * HEAD,), jnp.float32, -0.5, 0.5) * block_scale(seeds[7], (4 * D + 2 * HEAD,), ((0, 4),), -0.4, 0.0), -0.5, 0.5)
    in_first = gaussian(seeds[8], (D, HEADS * HEAD + 2 * HEAD), (0.1 * TOKENS ** 0.5), 112.0, ((0, 4),), jnp.float32)
    out_first = gaussian(seeds[9], (HEADS * HEAD, D), (0.1 * TOKENS ** 0.5), 112.0, ((0, 4),), jnp.float32)
    gate_first = gaussian(seeds[10], (D, 2 * FF), (0.1 * TOKENS ** 0.5), 112.0, ((0, 4),), jnp.float32)
    down_first = gaussian(seeds[11], (FF, D), (0.1 * TOKENS ** 0.5), 112.0, ((0, 4),), jnp.float32)
    gain_first = gaussian(seeds[12], (4 * D + 2 * HEAD,), (0.1 * TOKENS ** 0.5), 112.0, ((0, 4),), jnp.float32)
    in_second = jnp.clip(jnp.exp(math.log(9830.4) - 2.3025852 * jax.random.uniform(seeds[13], (D, HEADS * HEAD + 2 * HEAD), jnp.float32) ** block_scale(seeds[13], (D, HEADS * HEAD + 2 * HEAD), ((0, 4),), -0.2, 0.2)), 983.04, 9830.4)
    out_second = jnp.clip(jnp.exp(math.log(9830.4) - 2.3025852 * jax.random.uniform(seeds[14], (HEADS * HEAD, D), jnp.float32) ** block_scale(seeds[14], (HEADS * HEAD, D), ((0, 4),), -0.2, 0.2)), 983.04, 9830.4)
    gate_second = jnp.clip(jnp.exp(math.log(9830.4) - 2.3025852 * jax.random.uniform(seeds[15], (D, 2 * FF), jnp.float32) ** block_scale(seeds[15], (D, 2 * FF), ((0, 4),), -0.2, 0.2)), 983.04, 9830.4)
    down_second = jnp.clip(jnp.exp(math.log(9830.4) - 2.3025852 * jax.random.uniform(seeds[16], (FF, D), jnp.float32) ** block_scale(seeds[16], (FF, D), ((0, 4),), -0.2, 0.2)), 983.04, 9830.4)
    gain_second = jnp.clip(jnp.exp(math.log(9830.4) - 2.3025852 * jax.random.uniform(seeds[17], (4 * D + 2 * HEAD,), jnp.float32) ** block_scale(seeds[17], (4 * D + 2 * HEAD,), ((0, 4),), -0.2, 0.2)), 983.04, 9830.4)
    return dict(tokens=tokens, cotangent=cotangent, segment_ids=segment_ids, in_weight=in_weight, out_weight=out_weight, gate_weight=gate_weight, down_weight=down_weight, norm_gains=norm_gains, in_first=in_first, out_first=out_first, gate_first=gate_first, down_first=down_first, gain_first=gain_first, in_second=in_second, out_second=out_second, gate_second=gate_second, down_second=down_second, gain_second=gain_second)


EPS = 1e-06
THETA = 1000000.0
BETA_ONE = 0.9
BETA_TWO = 0.95
ADAM_EPS = 1e-08
DECAY_MATRIX = 0.1
RATE_MATRIX = 0.02
RATE_GAIN = 0.05

@jax.custom_vjp
def low(v):
    return lax.optimization_barrier(v.astype(jnp.bfloat16)).astype(jnp.float32)

@jax.custom_vjp
def low_back(v):
    return v

def low_keep(v):
    return (low(v), None)

def low_pass(kept, grad):
    return (grad,)

def back_keep(v):
    return (v, None)

def back_low(kept, grad):
    return (low(grad),)
low.defvjp(low_keep, low_pass)
low_back.defvjp(back_keep, back_low)

def rms_norm(vector, gain_vec):
    return vector * lax.rsqrt(lax.optimization_barrier(jnp.mean(vector * vector, -1, keepdims=True)) + EPS) * (1.0 + gain_vec)

def rotate(vector, cosine, sine_table):
    half_width = vector.shape[-1] // 2
    front_half = vector[..., :half_width]
    back_half = vector[..., half_width:]
    return jnp.concatenate([front_half * cosine - back_half * sine_table, back_half * cosine + front_half * sine_table], -1)

def segment_places(seg_row):
    row_count = seg_row.shape[0]
    places = jnp.arange(row_count, dtype=jnp.int32)
    starting = jnp.concatenate([jnp.ones((1,), bool), seg_row[1:] != seg_row[:-1]])
    firsts = lax.cummax(jnp.where(starting, places, jnp.zeros_like(places)), axis=0)
    return places - firsts

def rotary_tables(positions):
    half_width = HEAD // 2
    places = positions.astype(jnp.float32)
    inverse = jnp.power(THETA, -2.0 * jnp.arange(half_width, dtype=jnp.float32) / HEAD)
    angles = places[:, None] * inverse[None, :]
    return (jnp.cos(angles), jnp.sin(angles))

def block_forward(stream, seg_row, in_low, out_low, gate_low, down_low, gain_low):
    highest = lax.Precision.HIGHEST
    row_count = stream.shape[0]
    width = stream.shape[1]
    pre_attn = gain_low[0:width]
    post_attn = gain_low[width:2 * width]
    pre_ffn = gain_low[2 * width:3 * width]
    post_ffn = gain_low[3 * width:4 * width]
    query_gain = gain_low[4 * width:4 * width + HEAD]
    key_gain = gain_low[4 * width + HEAD:]
    query_cols = HEADS * HEAD
    normed = low(rms_norm(stream, pre_attn))
    projected = low_back(jnp.dot(normed, in_low, precision=highest))
    queries = projected[:, :query_cols].reshape(row_count, HEADS, HEAD)
    key_rows = projected[:, query_cols:query_cols + HEAD]
    values = projected[:, query_cols + HEAD:]
    cosine, sine_table = rotary_tables(segment_places(seg_row))
    queries = low(rotate(rms_norm(queries, query_gain), cosine[:, None, :], sine_table[:, None, :]))
    key_rows = low(rotate(rms_norm(key_rows, key_gain), cosine, sine_table))
    values = low(values)
    scores = jnp.einsum('thd,sd->hts', queries, key_rows, precision=highest) * HEAD ** (-0.5)
    scores = low_back(scores)
    places = jnp.arange(row_count, dtype=jnp.int32)
    visible = (places[None, :] <= places[:, None]) & (seg_row[None, :] == seg_row[:, None])
    scores = jnp.where(visible[None], scores, -1e+30)
    row_max = lax.optimization_barrier(jnp.max(scores, -1, keepdims=True))
    expo_scores = jnp.exp(scores - row_max)
    softmax_w = low(expo_scores / lax.optimization_barrier(jnp.sum(expo_scores, -1, keepdims=True)))
    mixed = jnp.einsum('hts,sd->thd', softmax_w, values, precision=highest).reshape(row_count, query_cols)
    mixed = low(low_back(mixed))
    attended = low_back(jnp.dot(mixed, out_low, precision=highest))
    resid = stream + rms_norm(attended, post_attn)
    fed = low(rms_norm(resid, pre_ffn))
    gated = low_back(jnp.dot(fed, gate_low, precision=highest))
    hidden = low(jax.nn.gelu(gated[:, :FF], approximate=True) * gated[:, FF:])
    lowered = low_back(jnp.dot(hidden, down_low, precision=highest))
    return resid + rms_norm(lowered, post_ffn)

def adamw(weight, gradient, moment_one, moment_two, rate, decay):
    moment_one = BETA_ONE * moment_one + (1.0 - BETA_ONE) * gradient
    moment_two = BETA_TWO * moment_two + (1.0 - BETA_TWO) * gradient * gradient
    corr_one = 1.0 - BETA_ONE ** STEP
    corr_two = 1.0 - BETA_TWO ** STEP
    update = moment_one / corr_one / (jnp.sqrt(moment_two / corr_two) + ADAM_EPS)
    weight = weight - rate * (update + decay * weight)
    return (weight, moment_one, moment_two)

def reference(tokens, cotangent, segment_ids, in_weight, out_weight, gate_weight, down_weight, norm_gains, in_first, out_first, gate_first, down_first, gain_first, in_second, out_second, gate_second, down_second, gain_second):
    groups = TOKENS // TOK_DEV
    stream_all = tokens.astype(jnp.float32).reshape(groups, TOK_DEV, D)
    cot_all = cotangent.astype(jnp.float32).reshape(groups, TOK_DEV, D)
    seg_all = segment_ids.reshape(groups, TOK_DEV)

    def total_loss(streams, in_w, out_w, gate_w, down_w, gains):
        in_low = low(in_w)
        out_low = low(out_w)
        gate_low = low(gate_w)
        down_low = low(down_w)
        gain_low = low(gains)
        checked = jax.checkpoint(block_forward)

        def per_device(carry, item):
            stream, cot_rows, seg_row = item
            result = checked(stream, seg_row, in_low, out_low, gate_low, down_low, gain_low)
            is_live = (seg_row >= 0).astype(jnp.float32)
            return (carry + jnp.sum(result * cot_rows * is_live[:, None]), result)
        loss_sum, results = lax.scan(per_device, jnp.zeros((), jnp.float32), (streams, cot_all, seg_all))
        return (loss_sum, results)
    loss_sum, pullback, results = jax.vjp(total_loss, stream_all, in_weight, out_weight, gate_weight, down_weight, norm_gains, has_aux=True)
    grads = pullback(jnp.ones((), jnp.float32))
    layer_out = results.reshape(TOKENS, D).astype(jnp.bfloat16)
    grad_input = grads[0].reshape(TOKENS, D).astype(jnp.bfloat16)
    new_in, in_momentum, in_variance = adamw(in_weight, grads[1], in_first, in_second, RATE_MATRIX, DECAY_MATRIX)
    new_out, out_momentum, out_variance = adamw(out_weight, grads[2], out_first, out_second, RATE_MATRIX, DECAY_MATRIX)
    new_gate, gate_momentum, gate_variance = adamw(gate_weight, grads[3], gate_first, gate_second, RATE_MATRIX, DECAY_MATRIX)
    new_down, down_momentum, down_variance = adamw(down_weight, grads[4], down_first, down_second, RATE_MATRIX, DECAY_MATRIX)
    new_gains, gain_momentum, gain_variance = adamw(norm_gains, grads[5], gain_first, gain_second, RATE_GAIN, 0.0)
    return (layer_out, grad_input, new_in, new_out, new_gate, new_down, new_gains, in_momentum, out_momentum, gate_momentum, down_momentum, gain_momentum, in_variance, out_variance, gate_variance, down_variance, gain_variance)
```

```python
from functools import partial

import jax
import jax.numpy as jnp
from jax import lax
from jax.sharding import PartitionSpec as P

HEADS = 4
HEAD = 256
FF = 2048
STEP = 10


EPS = 1e-06
THETA = 1000000.0
BETA_ONE = 0.9
BETA_TWO = 0.95
ADAM_EPS = 1e-08
DECAY_MATRIX = 0.1
RATE_MATRIX = 0.02
RATE_GAIN = 0.05


def rms_norm(vector, gain_vec):
    return vector * lax.rsqrt(jnp.mean(vector * vector, -1, keepdims=True) + EPS) * (1.0 + gain_vec)


def rotate(vector, cosine, sine_table):
    half_width = vector.shape[-1] // 2
    front_half = vector[..., :half_width]
    back_half = vector[..., half_width:]
    return jnp.concatenate(
        [
            front_half * cosine - back_half * sine_table,
            back_half * cosine + front_half * sine_table,
        ],
        -1,
    )


def segment_places(seg_row):
    row_count = seg_row.shape[0]
    places = jnp.arange(row_count, dtype=jnp.int32)
    starting = jnp.concatenate([jnp.ones((1,), bool), seg_row[1:] != seg_row[:-1]])
    firsts = lax.cummax(jnp.where(starting, places, jnp.zeros_like(places)), axis=0)
    return places - firsts


def rotary_tables(positions):
    half_width = HEAD // 2
    places = positions.astype(jnp.float32)
    inverse = jnp.power(THETA, -2.0 * jnp.arange(half_width, dtype=jnp.float32) / HEAD)
    angles = places[:, None] * inverse[None, :]
    return (jnp.cos(angles), jnp.sin(angles))


def query_prep(raw_rows, gain_vec, cosine, sine_table):
    return rotate(rms_norm(raw_rows, gain_vec), cosine[:, None, :], sine_table[:, None, :])


def key_prep(raw_rows, gain_vec, cosine, sine_table):
    return rotate(rms_norm(raw_rows, gain_vec), cosine, sine_table)


def geglu(gate_part, up_part):
    return jax.nn.gelu(gate_part, approximate=True) * up_part


def adamw(weight, gradient, moment_one, moment_two, rate, decay):
    moment_one = BETA_ONE * moment_one + (1.0 - BETA_ONE) * gradient
    moment_two = BETA_TWO * moment_two + (1.0 - BETA_TWO) * gradient * gradient
    corr_one = 1.0 - BETA_ONE**STEP
    corr_two = 1.0 - BETA_TWO**STEP
    update = moment_one / corr_one / (jnp.sqrt(moment_two / corr_two) + ADAM_EPS)
    weight = weight - rate * (update + decay * weight)
    return (weight, moment_one, moment_two)


def flip_pairs(axis_name, axis_size, bit):
    return [(place, place ^ bit) for place in range(axis_size)]


def exchange(array, axis_name, axis_size, bit):
    return lax.ppermute(array, axis_name, flip_pairs(axis_name, axis_size, bit))


def add_low(first, second):
    return (first.astype(jnp.float32) + second.astype(jnp.float32)).astype(first.dtype)


def gather_shards(piece, shards):
    index = lax.axis_index("shard")
    bit = shards // 2
    stack = piece[None]
    while bit:
        other = exchange(stack, "shard", shards, bit)
        high = (index & bit) != 0
        lower = jnp.where(high, other, stack)
        upper = jnp.where(high, stack, other)
        stack = jnp.concatenate([lower[:, None], upper[:, None]], 1)
        stack = stack.reshape((-1,) + piece.shape)
        bit //= 2
    return stack.reshape((-1,) + piece.shape[1:])


def scatter_shards(whole, shards):
    index = lax.axis_index("shard")
    piece = whole.reshape((shards, whole.shape[0] // shards) + whole.shape[1:])
    bit = 1
    while bit < shards:
        pairs = piece.reshape((piece.shape[0] // 2, 2) + piece.shape[1:])
        side = (index & bit) // bit
        keep = lax.dynamic_index_in_dim(pairs, side, 1, keepdims=False)
        send = lax.dynamic_index_in_dim(pairs, 1 - side, 1, keepdims=False)
        piece = add_low(keep, exchange(send, "shard", shards, bit))
        bit *= 2
    return piece[0]


def split_axis(shape):
    if shape[1] % 256 == 0:
        return 1
    if shape[0] % 2 == 0:
        return 0
    return 1


def sum_groups(piece, groups, bits):
    index = lax.axis_index("dp")
    axes = []
    for bit in bits:
        axis = split_axis(piece.shape)
        half = piece.shape[axis] // 2
        side = (index & bit) // bit
        keep = lax.dynamic_slice_in_dim(piece, side * half, half, axis)
        send = lax.dynamic_slice_in_dim(piece, (1 - side) * half, half, axis)
        piece = add_low(keep, exchange(send, "dp", groups, bit))
        axes.append(axis)
    for bit, axis in zip(reversed(bits), reversed(axes)):
        other = exchange(piece, "dp", groups, bit)
        high = (index & bit) != 0
        piece = jnp.concatenate(
            [jnp.where(high, other, piece), jnp.where(high, piece, other)], axis
        )
    return piece


def sum_small(piece, groups, bits):
    for bit in bits:
        piece = piece + exchange(piece, "dp", groups, bit)
    return piece


def group_bits(groups, swapped):
    bits = []
    bit = 1
    while bit < groups:
        bits.append(bit)
        bit *= 2
    if swapped and len(bits) > 1:
        bits[0], bits[1] = bits[1], bits[0]
    return bits


def body(
    tokens,
    cotangent,
    segment_ids,
    in_weight,
    out_weight,
    gate_weight,
    down_weight,
    norm_gains,
    in_first,
    out_first,
    gate_first,
    down_first,
    gain_first,
    in_second,
    out_second,
    gate_second,
    down_second,
    gain_second,
    *,
    groups,
    shards,
):
    row_count = tokens.shape[0]
    width = tokens.shape[1]
    query_cols = HEADS * HEAD
    score_scale = HEAD ** (-0.5)
    places = jnp.arange(row_count, dtype=jnp.int32)
    is_live = segment_ids >= 0
    in_full = gather_shards(in_weight.astype(jnp.bfloat16), shards)
    gain_low = gather_shards(norm_gains.astype(jnp.bfloat16).reshape(1, -1), shards).reshape(-1)
    out_full = gather_shards(out_weight.astype(jnp.bfloat16), shards)
    gate_full = gather_shards(gate_weight.astype(jnp.bfloat16), shards)
    down_full = gather_shards(down_weight.astype(jnp.bfloat16), shards)
    gain_full = gain_low.astype(jnp.float32)
    pre_attn = gain_full[0:width]
    post_attn = gain_full[width : 2 * width]
    pre_ffn = gain_full[2 * width : 3 * width]
    post_ffn = gain_full[3 * width : 4 * width]
    query_gain = gain_full[4 * width : 4 * width + HEAD]
    key_gain = gain_full[4 * width + HEAD :]
    stream = tokens.astype(jnp.float32)
    normed, pre_attn_back = jax.vjp(rms_norm, stream, pre_attn)
    normed_low = normed.astype(jnp.bfloat16)
    projected = jnp.dot(normed_low, in_full, preferred_element_type=jnp.float32)
    query_raw = projected[:, :query_cols].reshape(row_count, HEADS, HEAD)
    key_raw = projected[:, query_cols : query_cols + HEAD]
    value_raw = projected[:, query_cols + HEAD :]
    cosine, sine_table = rotary_tables(segment_places(segment_ids))
    queries, query_back = jax.vjp(
        partial(query_prep, cosine=cosine, sine_table=sine_table), query_raw, query_gain
    )
    key_rows, key_back = jax.vjp(
        partial(key_prep, cosine=cosine, sine_table=sine_table), key_raw, key_gain
    )
    query_low = queries.astype(jnp.bfloat16)
    key_low = key_rows.astype(jnp.bfloat16)
    value_low = value_raw.astype(jnp.bfloat16)
    block_rows = min(512, row_count)
    block_total = row_count // block_rows

    def visible_rows(row_start):
        row_stop = row_start + block_rows
        rows_here = places[row_start:row_stop]
        seg_here = segment_ids[row_start:row_stop]
        return (places[None, :row_stop] <= rows_here[:, None]) & (
            segment_ids[None, :row_stop] == seg_here[:, None]
        )

    def block_scores(block_index):
        row_start = block_index * block_rows
        query_block = query_low[row_start : row_start + block_rows]
        key_block = key_low[: row_start + block_rows]
        scores = (
            jnp.einsum("thd,sd->hts", query_block, key_block, preferred_element_type=jnp.float32)
            * score_scale
        )
        scores = jnp.where(visible_rows(row_start)[None], scores, -1e30)
        return (query_block, scores)

    def attend_block(block_index):
        query_block, scores = block_scores(block_index)
        row_max = jnp.max(scores, -1, keepdims=True)
        expo_scores = jnp.exp(scores - row_max)
        row_total = jnp.sum(expo_scores, -1, keepdims=True)
        softmax_w = (expo_scores / row_total).astype(jnp.bfloat16)
        mixed = jnp.einsum("hts,sd->thd", softmax_w, value_low[: softmax_w.shape[-1]], preferred_element_type=jnp.float32)
        return (mixed, row_max + jnp.log(row_total))

    blocks = [attend_block(block_index) for block_index in range(block_total)]
    log_totals = [block[1] for block in blocks]
    mixed_low = jnp.concatenate([block[0].astype(jnp.bfloat16) for block in blocks], 0)
    mixed_low = mixed_low.reshape(row_count, query_cols)
    attended = jnp.dot(mixed_low, out_full, preferred_element_type=jnp.float32)
    post_a, post_attn_back = jax.vjp(rms_norm, attended, post_attn)
    resid = stream + post_a
    fed, pre_ffn_back = jax.vjp(rms_norm, resid, pre_ffn)
    fed_low = fed.astype(jnp.bfloat16)
    gated = jnp.dot(fed_low, gate_full, preferred_element_type=jnp.float32)
    hidden, geglu_back = jax.vjp(geglu, gated[:, :FF], gated[:, FF:])
    hidden_low = hidden.astype(jnp.bfloat16)
    lowered = jnp.dot(hidden_low, down_full, preferred_element_type=jnp.float32)
    post_f, post_ffn_back = jax.vjp(rms_norm, lowered, post_ffn)
    layer_out = (resid + post_f).astype(jnp.bfloat16)
    grad_out_rows = cotangent.astype(jnp.float32) * is_live[:, None].astype(jnp.float32)
    grad_lowered, grad_post_ffn = post_ffn_back(grad_out_rows)
    grad_lowered = grad_lowered.astype(jnp.bfloat16)
    grad_down = jnp.einsum(
        "tf,td->fd", hidden_low, grad_lowered, preferred_element_type=jnp.float32
    )
    grad_hidden = jnp.einsum(
        "td,fd->tf", grad_lowered, down_full, preferred_element_type=jnp.float32
    )
    grad_gatepart, grad_uppart = geglu_back(grad_hidden)
    grad_gated = jnp.concatenate([grad_gatepart, grad_uppart], -1).astype(jnp.bfloat16)
    grad_gate = jnp.einsum("td,tf->df", fed_low, grad_gated, preferred_element_type=jnp.float32)
    grad_fed = jnp.einsum("tf,df->td", grad_gated, gate_full, preferred_element_type=jnp.float32)
    grad_resid_norm, grad_pre_ffn = pre_ffn_back(grad_fed)
    grad_resid = grad_out_rows + grad_resid_norm
    grad_attended, grad_post_attn = post_attn_back(grad_resid)
    grad_attended = grad_attended.astype(jnp.bfloat16)
    grad_attended, grad_down_low, grad_gate_low = lax.optimization_barrier(
        (grad_attended, grad_down.astype(jnp.bfloat16), grad_gate.astype(jnp.bfloat16))
    )
    plain_bits = group_bits(groups, False)
    swapped_bits = group_bits(groups, True)
    sum_gate = sum_groups(scatter_shards(grad_gate_low, shards), groups, plain_bits)
    sum_down = sum_groups(scatter_shards(grad_down_low, shards), groups, swapped_bits)
    grad_outw = jnp.einsum(
        "tk,td->kd", mixed_low, grad_attended, preferred_element_type=jnp.float32
    )
    grad_mixed = jnp.einsum(
        "td,kd->tk", grad_attended, out_full, preferred_element_type=jnp.float32
    )
    grad_mixed = grad_mixed.astype(jnp.bfloat16).reshape(row_count, HEADS, HEAD)
    grad_mixed, grad_out_low = lax.optimization_barrier(
        (grad_mixed, grad_outw.astype(jnp.bfloat16))
    )
    sum_out = sum_groups(scatter_shards(grad_out_low, shards), groups, swapped_bits)

    def back_block(block_index):
        row_start = block_index * block_rows
        row_stop = row_start + block_rows
        query_block, scores = block_scores(block_index)
        softmax_w = jnp.exp(scores - log_totals[block_index])
        grad_block = grad_mixed[row_start:row_stop]
        grad_val = jnp.einsum(
            "hts,thd->sd",
            softmax_w.astype(jnp.bfloat16),
            grad_block,
            preferred_element_type=jnp.float32,
        )
        grad_probs = jnp.einsum(
            "thd,sd->hts", grad_block, value_low[:row_stop], preferred_element_type=jnp.float32
        )
        row_delta = jnp.sum(softmax_w * grad_probs, -1, keepdims=True)
        grad_scores = (softmax_w * (grad_probs - row_delta)).astype(jnp.bfloat16)
        grad_query = (
            jnp.einsum(
                "hts,sd->thd", grad_scores, key_low[:row_stop], preferred_element_type=jnp.float32
            )
            * score_scale
        )
        grad_key = (
            jnp.einsum("hts,thd->sd", grad_scores, query_block, preferred_element_type=jnp.float32)
            * score_scale
        )
        fill = ((0, row_count - row_stop), (0, 0))
        return (jnp.pad(grad_key, fill), jnp.pad(grad_val, fill), grad_query)

    back_blocks = [back_block(block_index) for block_index in range(block_total)]
    grad_keyrows = sum(block[0] for block in back_blocks)
    grad_values = sum(block[1] for block in back_blocks)
    grad_queries = jnp.concatenate([block[2] for block in back_blocks], 0)
    grad_queries = grad_queries.reshape(row_count, HEADS, HEAD)
    grad_query_raw, grad_query_gain = query_back(grad_queries)
    grad_key_raw, grad_key_gain = key_back(grad_keyrows)
    grad_projected = jnp.concatenate(
        [grad_query_raw.reshape(row_count, query_cols), grad_key_raw, grad_values], -1
    ).astype(jnp.bfloat16)
    grad_inw = jnp.einsum(
        "td,tk->dk", normed_low, grad_projected, preferred_element_type=jnp.float32
    )
    grad_normed = jnp.einsum(
        "tk,dk->td", grad_projected, in_full, preferred_element_type=jnp.float32
    )
    grad_stream_norm, grad_pre_attn = pre_attn_back(grad_normed)
    grad_input = (grad_resid + grad_stream_norm).astype(jnp.bfloat16)
    grad_gains = jnp.concatenate(
        [
            grad_pre_attn,
            grad_post_attn,
            grad_pre_ffn,
            grad_post_ffn,
            grad_query_gain,
            grad_key_gain,
        ],
        0,
    )
    sum_in = sum_groups(scatter_shards(grad_inw.astype(jnp.bfloat16), shards), groups, plain_bits)
    sum_gains = sum_small(
        scatter_shards(grad_gains.reshape(shards, -1), shards), groups, plain_bits
    ).reshape(-1)
    sum_in, sum_out, sum_gate, sum_down = (
        part.astype(jnp.float32) for part in (sum_in, sum_out, sum_gate, sum_down)
    )
    new_in, in_momentum, in_variance = adamw(
        in_weight, sum_in, in_first, in_second, RATE_MATRIX, DECAY_MATRIX
    )
    new_out, out_momentum, out_variance = adamw(
        out_weight, sum_out, out_first, out_second, RATE_MATRIX, DECAY_MATRIX
    )
    new_gate, gate_momentum, gate_variance = adamw(
        gate_weight, sum_gate, gate_first, gate_second, RATE_MATRIX, DECAY_MATRIX
    )
    new_down, down_momentum, down_variance = adamw(
        down_weight, sum_down, down_first, down_second, RATE_MATRIX, DECAY_MATRIX
    )
    new_gains, gain_momentum, gain_variance = adamw(
        norm_gains, sum_gains, gain_first, gain_second, RATE_GAIN, 0.0
    )
    return (
        layer_out,
        grad_input,
        new_in,
        new_out,
        new_gate,
        new_down,
        new_gains,
        in_momentum,
        out_momentum,
        gate_momentum,
        down_momentum,
        gain_momentum,
        in_variance,
        out_variance,
        gate_variance,
        down_variance,
        gain_variance,
    )


def solution(mesh):
    in_specs = (
        P(("dp", "shard"), None),
        P(("dp", "shard"), None),
        P(("dp", "shard")),
        P("shard", None),
        P("shard", None),
        P("shard", None),
        P("shard", None),
        P("shard"),
        P("shard", None),
        P("shard", None),
        P("shard", None),
        P("shard", None),
        P("shard"),
        P("shard", None),
        P("shard", None),
        P("shard", None),
        P("shard", None),
        P("shard"),
    )
    out_specs = (
        P(("dp", "shard"), None),
        P(("dp", "shard"), None),
        P("shard", None),
        P("shard", None),
        P("shard", None),
        P("shard", None),
        P("shard"),
        P("shard", None),
        P("shard", None),
        P("shard", None),
        P("shard", None),
        P("shard"),
        P("shard", None),
        P("shard", None),
        P("shard", None),
        P("shard", None),
        P("shard"),
    )
    local = partial(body, groups=mesh.shape["dp"], shards=mesh.shape["shard"])
    return jax.shard_map(local, mesh=mesh, in_specs=in_specs, out_specs=out_specs, check_vma=False)
```

```python
from functools import partial

import jax
import jax.numpy as jnp
from jax import lax
from jax.sharding import PartitionSpec as P

HEADS = 4
HEAD = 256
FF = 2048
STEP = 10


EPS = 1e-06
THETA = 1000000.0
BETA_ONE = 0.9
BETA_TWO = 0.95
ADAM_EPS = 1e-08
DECAY_MATRIX = 0.1
RATE_MATRIX = 0.02
RATE_GAIN = 0.05


def rms_norm(vector, gain_vec):
    return vector * lax.rsqrt(jnp.mean(vector * vector, -1, keepdims=True) + EPS) * (1.0 + gain_vec)


def rotate(vector, cosine, sine_table):
    half_width = vector.shape[-1] // 2
    front_half = vector[..., :half_width]
    back_half = vector[..., half_width:]
    return jnp.concatenate(
        [
            front_half * cosine - back_half * sine_table,
            back_half * cosine + front_half * sine_table,
        ],
        -1,
    )


def segment_places(seg_row):
    row_count = seg_row.shape[0]
    places = jnp.arange(row_count, dtype=jnp.int32)
    starting = jnp.concatenate([jnp.ones((1,), bool), seg_row[1:] != seg_row[:-1]])
    firsts = lax.cummax(jnp.where(starting, places, jnp.zeros_like(places)), axis=0)
    return places - firsts


def rotary_tables(positions):
    half_width = HEAD // 2
    places = positions.astype(jnp.float32)
    inverse = jnp.power(THETA, -2.0 * jnp.arange(half_width, dtype=jnp.float32) / HEAD)
    angles = places[:, None] * inverse[None, :]
    return (jnp.cos(angles), jnp.sin(angles))


def query_prep(raw_rows, gain_vec, cosine, sine_table):
    return rotate(rms_norm(raw_rows, gain_vec), cosine[None], sine_table[None])


def key_prep(raw_rows, gain_vec, cosine, sine_table):
    return rotate(rms_norm(raw_rows, gain_vec), cosine, sine_table)


def split_heads(rows):
    return jnp.stack([rows[:, HEAD * head : HEAD * (head + 1)] for head in range(HEADS)])


def merge_heads(stack):
    return jnp.concatenate([stack[head] for head in range(HEADS)], -1)


def geglu(gate_part, up_part):
    return jax.nn.gelu(gate_part, approximate=True) * up_part


def adamw(weight, gradient, moment_one, moment_two, rate, decay):
    moment_one = BETA_ONE * moment_one + (1.0 - BETA_ONE) * gradient
    moment_two = BETA_TWO * moment_two + (1.0 - BETA_TWO) * gradient * gradient
    corr_one = 1.0 - BETA_ONE**STEP
    corr_two = 1.0 - BETA_TWO**STEP
    update = moment_one / corr_one / (jnp.sqrt(moment_two / corr_two) + ADAM_EPS)
    weight = weight - rate * (update + decay * weight)
    return (weight, moment_one, moment_two)


def flip_pairs(axis_name, axis_size, bit):
    return [(place, place ^ bit) for place in range(axis_size)]


def exchange(array, axis_name, axis_size, bit):
    return lax.ppermute(array, axis_name, flip_pairs(axis_name, axis_size, bit))


def add_low(first, second):
    return (first.astype(jnp.float32) + second.astype(jnp.float32)).astype(first.dtype)


def join_sides(stack, other, high, shape):
    lower = jnp.where(high, other, stack)
    upper = jnp.where(high, stack, other)
    joined = jnp.concatenate([lower[:, None], upper[:, None]], 1)
    return joined.reshape((-1,) + shape)


def gather_steps(piece, shards):
    index = lax.axis_index("shard")
    bit = shards // 2
    stack = piece[None]
    while bit:
        other = yield exchange(stack, "shard", shards, bit)
        stack = join_sides(stack, other, (index & bit) != 0, piece.shape)
        bit //= 2
    return stack.reshape((-1,) + piece.shape[1:])


def scatter_steps(whole, shards):
    index = lax.axis_index("shard")
    piece = whole.reshape((shards, whole.shape[0] // shards) + whole.shape[1:])
    bit = 1
    while bit < shards:
        pairs = piece.reshape((piece.shape[0] // 2, 2) + piece.shape[1:])
        side = (index & bit) // bit
        keep = lax.dynamic_index_in_dim(pairs, side, 1, keepdims=False)
        send = lax.dynamic_index_in_dim(pairs, 1 - side, 1, keepdims=False)
        other = yield exchange(send, "shard", shards, bit)
        piece = add_low(keep, other)
        bit *= 2
    return piece[0]


def split_axis(shape):
    if shape[1] % 256 == 0:
        return 1
    if shape[0] % 2 == 0:
        return 0
    return 1


def group_steps(piece, groups, bits):
    index = lax.axis_index("dp")
    axes = []
    for bit in bits:
        axis = split_axis(piece.shape)
        half = piece.shape[axis] // 2
        side = (index & bit) // bit
        keep = lax.dynamic_slice_in_dim(piece, side * half, half, axis)
        send = lax.dynamic_slice_in_dim(piece, (1 - side) * half, half, axis)
        other = yield exchange(send, "dp", groups, bit)
        piece = add_low(keep, other)
        axes.append(axis)
    for bit, axis in zip(reversed(bits), reversed(axes)):
        other = yield exchange(piece, "dp", groups, bit)
        high = (index & bit) != 0
        piece = jnp.concatenate(
            [jnp.where(high, other, piece), jnp.where(high, piece, other)], axis
        )
    return piece


def matrix_steps(whole, shards, groups, bits):
    piece = yield from scatter_steps(whole, shards)
    return (yield from group_steps(piece, groups, bits))


def gain_steps(whole, shards, groups, bits):
    piece = yield from scatter_steps(whole, shards)
    for bit in bits:
        piece = piece + (yield exchange(piece, "dp", groups, bit))
    return piece


class Chain:
    def __init__(self, steps):
        self.steps = steps
        self.result = None
        self.arrived = None
        self.advance(None)

    def advance(self, arrived):
        try:
            self.arrived = self.steps.send(arrived)
        except StopIteration as stop:
            self.arrived = None
            self.result = stop.value

    def finish(self):
        while self.result is None:
            self.advance(self.arrived)
        return self.result


def tie(values, chains):
    chains = [chain for chain in chains if chain.result is None]
    count = len(values)
    tied = lax.optimization_barrier(
        tuple(values) + tuple(chain.arrived for chain in chains)
    )
    for chain, arrived in zip(chains, tied[count:]):
        chain.advance(arrived)
    return tied[:count]


def group_bits(groups, swapped):
    bits = []
    bit = 1
    while bit < groups:
        bits.append(bit)
        bit *= 2
    if swapped and len(bits) > 1:
        bits[0], bits[1] = bits[1], bits[0]
    return bits


def body(
    tokens,
    cotangent,
    segment_ids,
    in_weight,
    out_weight,
    gate_weight,
    down_weight,
    norm_gains,
    in_first,
    out_first,
    gate_first,
    down_first,
    gain_first,
    in_second,
    out_second,
    gate_second,
    down_second,
    gain_second,
    *,
    groups,
    shards,
):
    row_count = tokens.shape[0]
    width = tokens.shape[1]
    query_cols = HEADS * HEAD
    score_scale = HEAD ** (-0.5)
    places = jnp.arange(row_count, dtype=jnp.int32)
    is_live = segment_ids >= 0
    in_chain = Chain(gather_steps(in_weight.astype(jnp.bfloat16), shards))
    gain_chain = Chain(gather_steps(norm_gains.astype(jnp.bfloat16).reshape(1, -1), shards))
    (out_piece,) = tie((out_weight.astype(jnp.bfloat16),), (in_chain,))
    out_chain = Chain(gather_steps(out_piece, shards))
    gain_low = gain_chain.finish().reshape(-1)
    in_full = in_chain.finish()
    gain_full = gain_low.astype(jnp.float32)
    pre_attn = gain_full[0:width]
    post_attn = gain_full[width : 2 * width]
    pre_ffn = gain_full[2 * width : 3 * width]
    post_ffn = gain_full[3 * width : 4 * width]
    query_gain = gain_full[4 * width : 4 * width + HEAD]
    key_gain = gain_full[4 * width + HEAD :]
    stream = tokens.astype(jnp.float32)
    normed, pre_attn_back = jax.vjp(rms_norm, stream, pre_attn)
    normed_low = normed.astype(jnp.bfloat16)
    projected = jnp.dot(normed_low, in_full, preferred_element_type=jnp.float32)
    projected, gate_piece = tie((projected, gate_weight.astype(jnp.bfloat16)), (out_chain,))
    gate_chain = Chain(gather_steps(gate_piece, shards))
    query_raw = split_heads(projected[:, :query_cols])
    key_raw = projected[:, query_cols : query_cols + HEAD]
    value_raw = projected[:, query_cols + HEAD :]
    cosine, sine_table = rotary_tables(segment_places(segment_ids))
    queries, query_back = jax.vjp(
        partial(query_prep, cosine=cosine, sine_table=sine_table), query_raw, query_gain
    )
    key_rows, key_back = jax.vjp(
        partial(key_prep, cosine=cosine, sine_table=sine_table), key_raw, key_gain
    )
    query_low = queries.astype(jnp.bfloat16)
    key_low = key_rows.astype(jnp.bfloat16)
    value_low = value_raw.astype(jnp.bfloat16)
    block_rows = min(512, row_count)
    block_total = row_count // block_rows

    def visible_rows(row_start):
        row_stop = row_start + block_rows
        rows_here = places[row_start:row_stop]
        seg_here = segment_ids[row_start:row_stop]
        return (places[None, :row_stop] <= rows_here[:, None]) & (
            segment_ids[None, :row_stop] == seg_here[:, None]
        )

    def block_scores(block_index, query_rows):
        row_start = block_index * block_rows
        query_block = query_rows[:, row_start : row_start + block_rows]
        key_block = key_low[: row_start + block_rows]
        scores = (
            jnp.einsum("htd,sd->hts", query_block, key_block, preferred_element_type=jnp.float32)
            * score_scale
        )
        scores = jnp.where(visible_rows(row_start)[None], scores, -1e30)
        return (query_block, scores)

    def attend_block(block_index, query_rows):
        query_block, scores = block_scores(block_index, query_rows)
        row_max = jnp.max(scores, -1, keepdims=True)
        expo_scores = jnp.exp(scores - row_max)
        row_total = jnp.sum(expo_scores, -1, keepdims=True)
        softmax_w = (expo_scores / row_total).astype(jnp.bfloat16)
        mixed = jnp.einsum("hts,sd->htd", softmax_w, value_low[: softmax_w.shape[-1]], preferred_element_type=jnp.float32)
        return (mixed, row_max + jnp.log(row_total))

    blocks = []
    query_rows = query_low
    down_chain = None
    for block_index in range(block_total):
        blocks.append(attend_block(block_index, query_rows))
        if down_chain is None:
            query_rows, down_piece = tie(
                (query_rows, down_weight.astype(jnp.bfloat16)), (gate_chain,)
            )
            down_chain = Chain(gather_steps(down_piece, shards))
    log_totals = [block[1] for block in blocks]
    mixed_low = merge_heads(jnp.concatenate([block[0].astype(jnp.bfloat16) for block in blocks], 1))
    out_full = out_chain.finish()
    attended = jnp.dot(mixed_low, out_full, preferred_element_type=jnp.float32)
    post_a, post_attn_back = jax.vjp(rms_norm, attended, post_attn)
    resid = stream + post_a
    fed, pre_ffn_back = jax.vjp(rms_norm, resid, pre_ffn)
    fed_low = fed.astype(jnp.bfloat16)
    gate_full = gate_chain.finish()
    gated = jnp.dot(fed_low, gate_full, preferred_element_type=jnp.float32)
    hidden, geglu_back = jax.vjp(geglu, gated[:, :FF], gated[:, FF:])
    hidden_low = hidden.astype(jnp.bfloat16)
    down_full = down_chain.finish()
    lowered = jnp.dot(hidden_low, down_full, preferred_element_type=jnp.float32)
    post_f, post_ffn_back = jax.vjp(rms_norm, lowered, post_ffn)
    layer_out = (resid + post_f).astype(jnp.bfloat16)
    grad_out_rows = cotangent.astype(jnp.float32) * is_live[:, None].astype(jnp.float32)
    grad_lowered, grad_post_ffn = post_ffn_back(grad_out_rows)
    grad_lowered = grad_lowered.astype(jnp.bfloat16)
    plain_bits = group_bits(groups, False)
    swapped_bits = group_bits(groups, True)
    grad_down = jnp.einsum(
        "tf,td->fd", hidden_low, grad_lowered, preferred_element_type=jnp.float32
    )
    grad_lowered, grad_down = lax.optimization_barrier(
        (grad_lowered, grad_down.astype(jnp.bfloat16))
    )
    down_sum = Chain(matrix_steps(grad_down, shards, groups, swapped_bits))
    grad_hidden = jnp.einsum(
        "td,fd->tf", grad_lowered, down_full, preferred_element_type=jnp.float32
    )
    grad_gatepart, grad_uppart = geglu_back(grad_hidden)
    grad_gated = jnp.concatenate([grad_gatepart, grad_uppart], -1).astype(jnp.bfloat16)
    (grad_gated,) = tie((grad_gated,), (down_sum,))
    grad_gate = jnp.einsum("td,tf->df", fed_low, grad_gated, preferred_element_type=jnp.float32)
    grad_gated, grad_gate = lax.optimization_barrier((grad_gated, grad_gate.astype(jnp.bfloat16)))
    gate_sum = Chain(matrix_steps(grad_gate, shards, groups, plain_bits))
    grad_fed = jnp.einsum("tf,df->td", grad_gated, gate_full, preferred_element_type=jnp.float32)
    (grad_fed,) = tie((grad_fed,), (down_sum, gate_sum))
    grad_resid_norm, grad_pre_ffn = pre_ffn_back(grad_fed)
    grad_resid = grad_out_rows + grad_resid_norm
    grad_attended, grad_post_attn = post_attn_back(grad_resid)
    grad_attended = grad_attended.astype(jnp.bfloat16)
    grad_outw = jnp.einsum(
        "tk,td->kd", mixed_low, grad_attended, preferred_element_type=jnp.float32
    )
    grad_mixed = jnp.einsum(
        "td,kd->tk", grad_attended, out_full, preferred_element_type=jnp.float32
    )
    grad_mixed, grad_outw = tie(
        (grad_mixed.astype(jnp.bfloat16), grad_outw.astype(jnp.bfloat16)), (down_sum,)
    )
    out_sum = Chain(matrix_steps(grad_outw, shards, groups, swapped_bits))
    grad_mixed = split_heads(grad_mixed)

    def back_block(block_index, query_rows, grad_mixed):
        row_start = block_index * block_rows
        row_stop = row_start + block_rows
        query_block, scores = block_scores(block_index, query_rows)
        softmax_w = jnp.exp(scores - log_totals[block_index])
        grad_block = grad_mixed[:, row_start:row_stop]
        grad_val = jnp.einsum(
            "hts,htd->sd",
            softmax_w.astype(jnp.bfloat16),
            grad_block,
            preferred_element_type=jnp.float32,
        )
        grad_probs = jnp.einsum(
            "htd,sd->hts", grad_block, value_low[:row_stop], preferred_element_type=jnp.float32
        )
        row_delta = jnp.sum(softmax_w * grad_probs, -1, keepdims=True)
        grad_scores = (softmax_w * (grad_probs - row_delta)).astype(jnp.bfloat16)
        grad_query = (
            jnp.einsum(
                "hts,sd->htd", grad_scores, key_low[:row_stop], preferred_element_type=jnp.float32
            )
            * score_scale
        )
        grad_key = (
            jnp.einsum("hts,htd->sd", grad_scores, query_block, preferred_element_type=jnp.float32)
            * score_scale
        )
        fill = ((0, row_count - row_stop), (0, 0))
        return (jnp.pad(grad_key, fill), jnp.pad(grad_val, fill), grad_query)

    back_blocks = []
    for block_index in range(block_total):
        grad_key, grad_val, grad_query = back_block(block_index, query_low, grad_mixed)
        running = (down_sum, out_sum)
        if block_index == block_total - 1:
            running = (down_sum, out_sum, gate_sum)
        grad_key, grad_val, grad_query, query_low, grad_mixed = tie(
            (grad_key, grad_val, grad_query, query_low, grad_mixed), running
        )
        back_blocks.append((grad_key, grad_val, grad_query))
    grad_keyrows = sum(block[0] for block in back_blocks)
    grad_values = sum(block[1] for block in back_blocks)
    grad_queries = jnp.concatenate([block[2] for block in back_blocks], 1)
    grad_query_raw, grad_query_gain = query_back(grad_queries)
    grad_query_raw = merge_heads(grad_query_raw.astype(jnp.bfloat16))
    grad_key_raw, grad_key_gain = key_back(grad_keyrows)
    grad_projected = jnp.concatenate(
        [grad_query_raw, grad_key_raw.astype(jnp.bfloat16), grad_values.astype(jnp.bfloat16)], -1
    )
    (grad_projected,) = tie((grad_projected,), (down_sum, out_sum, gate_sum))
    grad_inw = jnp.einsum(
        "td,tk->dk", normed_low, grad_projected, preferred_element_type=jnp.float32
    )
    grad_projected, grad_inw = tie(
        (grad_projected, grad_inw.astype(jnp.bfloat16)), ()
    )
    in_sum = Chain(matrix_steps(grad_inw, shards, groups, plain_bits))
    grad_normed = jnp.einsum(
        "tk,dk->td", grad_projected, in_full, preferred_element_type=jnp.float32
    )
    grad_stream_norm, grad_pre_attn = pre_attn_back(grad_normed)
    grad_input = (grad_resid + grad_stream_norm).astype(jnp.bfloat16)
    grad_gains = jnp.concatenate(
        [
            grad_pre_attn,
            grad_post_attn,
            grad_pre_ffn,
            grad_post_ffn,
            grad_query_gain,
            grad_key_gain,
        ],
        0,
    )
    gain_sum = Chain(gain_steps(grad_gains.reshape(shards, -1), shards, groups, plain_bits))
    running = (down_sum, out_sum, gate_sum, in_sum, gain_sum)
    sum_down, sum_out, sum_gate, sum_in, sum_gains = (
        chain.finish().astype(jnp.float32) for chain in running
    )
    sum_gains = sum_gains.reshape(-1)
    new_in, in_momentum, in_variance = adamw(
        in_weight, sum_in, in_first, in_second, RATE_MATRIX, DECAY_MATRIX
    )
    new_out, out_momentum, out_variance = adamw(
        out_weight, sum_out, out_first, out_second, RATE_MATRIX, DECAY_MATRIX
    )
    new_gate, gate_momentum, gate_variance = adamw(
        gate_weight, sum_gate, gate_first, gate_second, RATE_MATRIX, DECAY_MATRIX
    )
    new_down, down_momentum, down_variance = adamw(
        down_weight, sum_down, down_first, down_second, RATE_MATRIX, DECAY_MATRIX
    )
    new_gains, gain_momentum, gain_variance = adamw(
        norm_gains, sum_gains, gain_first, gain_second, RATE_GAIN, 0.0
    )
    return (
        layer_out,
        grad_input,
        new_in,
        new_out,
        new_gate,
        new_down,
        new_gains,
        in_momentum,
        out_momentum,
        gate_momentum,
        down_momentum,
        gain_momentum,
        in_variance,
        out_variance,
        gate_variance,
        down_variance,
        gain_variance,
    )


def solution(mesh):
    in_specs = (
        P(("dp", "shard"), None),
        P(("dp", "shard"), None),
        P(("dp", "shard")),
        P("shard", None),
        P("shard", None),
        P("shard", None),
        P("shard", None),
        P("shard"),
        P("shard", None),
        P("shard", None),
        P("shard", None),
        P("shard", None),
        P("shard"),
        P("shard", None),
        P("shard", None),
        P("shard", None),
        P("shard", None),
        P("shard"),
    )
    out_specs = (
        P(("dp", "shard"), None),
        P(("dp", "shard"), None),
        P("shard", None),
        P("shard", None),
        P("shard", None),
        P("shard", None),
        P("shard"),
        P("shard", None),
        P("shard", None),
        P("shard", None),
        P("shard", None),
        P("shard"),
        P("shard", None),
        P("shard", None),
        P("shard", None),
        P("shard", None),
        P("shard"),
    )
    local = partial(body, groups=mesh.shape["dp"], shards=mesh.shape["shard"])
    return jax.shard_map(local, mesh=mesh, in_specs=in_specs, out_specs=out_specs, check_vma=False)
```

```python
from functools import partial

import jax
import jax.numpy as jnp
from jax import lax
from jax.sharding import PartitionSpec as P

HEADS = 4
HEAD = 256
FF = 2048
STEP = 10


EPS = 1e-06
THETA = 1000000.0
BETA_ONE = 0.9
BETA_TWO = 0.95
ADAM_EPS = 1e-08
DECAY_MATRIX = 0.1
RATE_MATRIX = 0.02
RATE_GAIN = 0.05


def rms_norm(vector, gain_vec):
    return vector * lax.rsqrt(jnp.mean(vector * vector, -1, keepdims=True) + EPS) * (1.0 + gain_vec)


def rotate(vector, cosine, sine_table):
    half_width = vector.shape[-1] // 2
    front_half = vector[..., :half_width]
    back_half = vector[..., half_width:]
    return jnp.concatenate(
        [
            front_half * cosine - back_half * sine_table,
            back_half * cosine + front_half * sine_table,
        ],
        -1,
    )


def segment_places(seg_row):
    row_count = seg_row.shape[0]
    places = jnp.arange(row_count, dtype=jnp.int32)
    starting = jnp.concatenate([jnp.ones((1,), bool), seg_row[1:] != seg_row[:-1]])
    firsts = lax.cummax(jnp.where(starting, places, jnp.zeros_like(places)), axis=0)
    return places - firsts


def rotary_tables(positions):
    half_width = HEAD // 2
    places = positions.astype(jnp.float32)
    inverse = jnp.power(THETA, -2.0 * jnp.arange(half_width, dtype=jnp.float32) / HEAD)
    angles = places[:, None] * inverse[None, :]
    return (jnp.cos(angles), jnp.sin(angles))


def query_prep(raw_rows, gain_vec, cosine, sine_table):
    return rotate(rms_norm(raw_rows, gain_vec), cosine[None], sine_table[None])


def key_prep(raw_rows, gain_vec, cosine, sine_table):
    return rotate(rms_norm(raw_rows, gain_vec), cosine, sine_table)


def split_heads(rows):
    return jnp.stack([rows[:, HEAD * head : HEAD * (head + 1)] for head in range(HEADS)])


def merge_heads(stack):
    return jnp.concatenate([stack[head] for head in range(HEADS)], -1)


def geglu(gate_part, up_part):
    return jax.nn.gelu(gate_part, approximate=True) * up_part


def adamw(weight, gradient, moment_one, moment_two, rate, decay):
    moment_one = BETA_ONE * moment_one + (1.0 - BETA_ONE) * gradient
    moment_two = BETA_TWO * moment_two + (1.0 - BETA_TWO) * gradient * gradient
    corr_one = 1.0 - BETA_ONE**STEP
    corr_two = 1.0 - BETA_TWO**STEP
    update = moment_one / corr_one / (jnp.sqrt(moment_two / corr_two) + ADAM_EPS)
    weight = weight - rate * (update + decay * weight)
    return (weight, moment_one, moment_two)


def flip_pairs(axis_name, axis_size, bit):
    return [(place, place ^ bit) for place in range(axis_size)]


def exchange(array, axis_name, axis_size, bit):
    return lax.ppermute(array, axis_name, flip_pairs(axis_name, axis_size, bit))


def add_low(first, second):
    return (first.astype(jnp.float32) + second.astype(jnp.float32)).astype(first.dtype)


def join_sides(stack, other, high, shape):
    lower = jnp.where(high, other, stack)
    upper = jnp.where(high, stack, other)
    joined = jnp.concatenate([lower[:, None], upper[:, None]], 1)
    return joined.reshape((-1,) + shape)


def gather_steps(piece, shards):
    index = lax.axis_index("shard")
    bit = shards // 2
    stack = piece[None]
    while bit:
        other = yield exchange(stack, "shard", shards, bit)
        stack = join_sides(stack, other, (index & bit) != 0, piece.shape)
        bit //= 2
    return stack.reshape((-1,) + piece.shape[1:])


def scatter_steps(whole, shards):
    index = lax.axis_index("shard")
    piece = whole.reshape((shards, whole.shape[0] // shards) + whole.shape[1:])
    bit = 1
    while bit < shards:
        pairs = piece.reshape((piece.shape[0] // 2, 2) + piece.shape[1:])
        side = (index & bit) // bit
        keep = lax.dynamic_index_in_dim(pairs, side, 1, keepdims=False)
        send = lax.dynamic_index_in_dim(pairs, 1 - side, 1, keepdims=False)
        other = yield exchange(send, "shard", shards, bit)
        piece = add_low(keep, other)
        bit *= 2
    return piece[0]


def split_axis(shape):
    if shape[1] % 256 == 0:
        return 1
    if shape[0] % 2 == 0:
        return 0
    return 1


def group_steps(piece, groups, bits):
    index = lax.axis_index("dp")
    axes = []
    for bit in bits:
        axis = split_axis(piece.shape)
        half = piece.shape[axis] // 2
        side = (index & bit) // bit
        keep = lax.dynamic_slice_in_dim(piece, side * half, half, axis)
        send = lax.dynamic_slice_in_dim(piece, (1 - side) * half, half, axis)
        other = yield exchange(send, "dp", groups, bit)
        piece = add_low(keep, other)
        axes.append(axis)
    for bit, axis in zip(reversed(bits), reversed(axes)):
        other = yield exchange(piece, "dp", groups, bit)
        high = (index & bit) != 0
        piece = jnp.concatenate(
            [jnp.where(high, other, piece), jnp.where(high, piece, other)], axis
        )
    return piece


def matrix_steps(whole, shards, groups, bits):
    piece = yield from scatter_steps(whole, shards)
    return (yield from group_steps(piece, groups, bits))


def gain_steps(whole, shards, groups, bits):
    piece = yield from scatter_steps(whole, shards)
    for bit in bits:
        piece = piece + (yield exchange(piece, "dp", groups, bit))
    return piece


class Chain:
    def __init__(self, steps):
        self.steps = steps
        self.result = None
        self.arrived = None
        self.advance(None)

    def advance(self, arrived):
        try:
            self.arrived = self.steps.send(arrived)
        except StopIteration as stop:
            self.arrived = None
            self.result = stop.value

    def finish(self):
        while self.result is None:
            self.advance(self.arrived)
        return self.result


def tie(values, chains):
    chains = [chain for chain in chains if chain.result is None]
    count = len(values)
    tied = lax.optimization_barrier(
        tuple(values) + tuple(chain.arrived for chain in chains)
    )
    for chain, arrived in zip(chains, tied[count:]):
        chain.advance(arrived)
    return tied[:count]


def group_bits(groups, swapped):
    bits = []
    bit = 1
    while bit < groups:
        bits.append(bit)
        bit *= 2
    if swapped and len(bits) > 1:
        bits[0], bits[1] = bits[1], bits[0]
    return bits


def body(
    tokens,
    cotangent,
    segment_ids,
    in_weight,
    out_weight,
    gate_weight,
    down_weight,
    norm_gains,
    in_first,
    out_first,
    gate_first,
    down_first,
    gain_first,
    in_second,
    out_second,
    gate_second,
    down_second,
    gain_second,
    *,
    groups,
    shards,
):
    row_count = tokens.shape[0]
    width = tokens.shape[1]
    query_cols = HEADS * HEAD
    score_scale = HEAD ** (-0.5)
    places = jnp.arange(row_count, dtype=jnp.int32)
    is_live = segment_ids >= 0
    in_chain = Chain(gather_steps(in_weight.astype(jnp.bfloat16), shards))
    gain_chain = Chain(gather_steps(norm_gains.astype(jnp.bfloat16).reshape(1, -1), shards))
    out_piece, gate_piece = tie(
        (out_weight.astype(jnp.bfloat16), gate_weight.astype(jnp.bfloat16)), (in_chain,)
    )
    out_chain = Chain(gather_steps(out_piece, shards))
    gate_chain = Chain(gather_steps(gate_piece, shards))
    gain_low = gain_chain.finish().reshape(-1)
    in_full = in_chain.finish()
    gain_full = gain_low.astype(jnp.float32)
    pre_attn = gain_full[0:width]
    post_attn = gain_full[width : 2 * width]
    pre_ffn = gain_full[2 * width : 3 * width]
    post_ffn = gain_full[3 * width : 4 * width]
    query_gain = gain_full[4 * width : 4 * width + HEAD]
    key_gain = gain_full[4 * width + HEAD :]
    stream = tokens.astype(jnp.float32)
    normed, pre_attn_back = jax.vjp(rms_norm, stream, pre_attn)
    normed_low = normed.astype(jnp.bfloat16)
    projected = jnp.dot(normed_low, in_full, preferred_element_type=jnp.float32)
    projected, down_piece = tie((projected, down_weight.astype(jnp.bfloat16)), (out_chain,))
    down_chain = Chain(gather_steps(down_piece, shards))
    query_raw = split_heads(projected[:, :query_cols])
    key_raw = projected[:, query_cols : query_cols + HEAD]
    value_raw = projected[:, query_cols + HEAD :]
    cosine, sine_table = rotary_tables(segment_places(segment_ids))
    queries, query_back = jax.vjp(
        partial(query_prep, cosine=cosine, sine_table=sine_table), query_raw, query_gain
    )
    key_rows, key_back = jax.vjp(
        partial(key_prep, cosine=cosine, sine_table=sine_table), key_raw, key_gain
    )
    query_low = queries.astype(jnp.bfloat16)
    key_low = key_rows.astype(jnp.bfloat16)
    value_low = value_raw.astype(jnp.bfloat16)
    block_rows = min(512, row_count)
    block_total = row_count // block_rows

    def visible_rows(row_start):
        row_stop = row_start + block_rows
        rows_here = places[row_start:row_stop]
        seg_here = segment_ids[row_start:row_stop]
        return (places[None, :row_stop] <= rows_here[:, None]) & (
            segment_ids[None, :row_stop] == seg_here[:, None]
        )

    def block_scores(block_index, query_rows):
        row_start = block_index * block_rows
        query_block = query_rows[:, row_start : row_start + block_rows]
        key_block = key_low[: row_start + block_rows]
        scores = (
            jnp.einsum("htd,sd->hts", query_block, key_block, preferred_element_type=jnp.float32)
            * score_scale
        )
        scores = jnp.where(visible_rows(row_start)[None], scores, -1e30)
        return (query_block, scores)

    def attend_block(block_index, query_rows):
        query_block, scores = block_scores(block_index, query_rows)
        row_max = jnp.max(scores, -1, keepdims=True)
        expo_scores = jnp.exp(scores - row_max)
        row_total = jnp.sum(expo_scores, -1, keepdims=True)
        softmax_w = (expo_scores / row_total).astype(jnp.bfloat16)
        mixed = jnp.einsum("hts,sd->htd", softmax_w, value_low[: softmax_w.shape[-1]], preferred_element_type=jnp.float32)
        return (mixed, row_max + jnp.log(row_total))

    blocks = []
    for block_index in range(block_total):
        blocks.append(attend_block(block_index, query_low))
    log_totals = [block[1] for block in blocks]
    mixed_low = merge_heads(jnp.concatenate([block[0].astype(jnp.bfloat16) for block in blocks], 1))
    (mixed_low,) = tie((mixed_low,), (gate_chain,))
    out_full = out_chain.finish()
    attended = jnp.dot(mixed_low, out_full, preferred_element_type=jnp.float32)
    post_a, post_attn_back = jax.vjp(rms_norm, attended, post_attn)
    resid = stream + post_a
    fed, pre_ffn_back = jax.vjp(rms_norm, resid, pre_ffn)
    fed_low = fed.astype(jnp.bfloat16)
    (fed_low,) = tie((fed_low,), (down_chain,))
    gate_full = gate_chain.finish()
    gated = jnp.dot(fed_low, gate_full, preferred_element_type=jnp.float32)
    hidden, geglu_back = jax.vjp(geglu, gated[:, :FF], gated[:, FF:])
    hidden_low = hidden.astype(jnp.bfloat16)
    down_full = down_chain.finish()
    lowered = jnp.dot(hidden_low, down_full, preferred_element_type=jnp.float32)
    post_f, post_ffn_back = jax.vjp(rms_norm, lowered, post_ffn)
    layer_out = (resid + post_f).astype(jnp.bfloat16)
    grad_out_rows = cotangent.astype(jnp.float32) * is_live[:, None].astype(jnp.float32)
    grad_lowered, grad_post_ffn = post_ffn_back(grad_out_rows)
    grad_lowered = grad_lowered.astype(jnp.bfloat16)
    plain_bits = group_bits(groups, False)
    swapped_bits = group_bits(groups, True)
    grad_down = jnp.einsum(
        "tf,td->fd", hidden_low, grad_lowered, preferred_element_type=jnp.float32
    )
    grad_lowered, grad_down = lax.optimization_barrier(
        (grad_lowered, grad_down.astype(jnp.bfloat16))
    )
    down_sum = Chain(matrix_steps(grad_down, shards, groups, swapped_bits))
    grad_hidden = jnp.einsum(
        "td,fd->tf", grad_lowered, down_full, preferred_element_type=jnp.float32
    )
    grad_gatepart, grad_uppart = geglu_back(grad_hidden)
    gated_parts = tie(
        (grad_gatepart.astype(jnp.bfloat16), grad_uppart.astype(jnp.bfloat16)), (down_sum,)
    )
    grad_gated = jnp.concatenate(gated_parts, -1)
    grad_gate = jnp.einsum("td,tf->df", fed_low, grad_gated, preferred_element_type=jnp.float32)
    *gated_parts, grad_gate = tie((*gated_parts, grad_gate.astype(jnp.bfloat16)), ())
    grad_gated = jnp.concatenate(gated_parts, -1)
    gate_sum = Chain(matrix_steps(grad_gate, shards, groups, plain_bits))
    grad_fed = jnp.einsum("tf,df->td", grad_gated, gate_full, preferred_element_type=jnp.float32)
    (grad_fed,) = tie((grad_fed,), (down_sum, gate_sum))
    grad_resid_norm, grad_pre_ffn = pre_ffn_back(grad_fed)
    grad_resid = grad_out_rows + grad_resid_norm
    grad_attended, grad_post_attn = post_attn_back(grad_resid)
    grad_attended = grad_attended.astype(jnp.bfloat16)
    grad_outw = jnp.einsum(
        "tk,td->kd", mixed_low, grad_attended, preferred_element_type=jnp.float32
    )
    grad_mixed = jnp.einsum(
        "td,kd->tk", grad_attended, out_full, preferred_element_type=jnp.float32
    )
    grad_mixed, grad_outw = tie(
        (grad_mixed.astype(jnp.bfloat16), grad_outw.astype(jnp.bfloat16)), (down_sum,)
    )
    out_sum = Chain(matrix_steps(grad_outw, shards, groups, swapped_bits))
    grad_mixed = split_heads(grad_mixed)

    def back_block(block_index, query_rows, grad_mixed):
        row_start = block_index * block_rows
        row_stop = row_start + block_rows
        query_block, scores = block_scores(block_index, query_rows)
        softmax_w = jnp.exp(scores - log_totals[block_index])
        grad_block = grad_mixed[:, row_start:row_stop]
        grad_val = jnp.einsum(
            "hts,htd->sd",
            softmax_w.astype(jnp.bfloat16),
            grad_block,
            preferred_element_type=jnp.float32,
        )
        grad_probs = jnp.einsum(
            "htd,sd->hts", grad_block, value_low[:row_stop], preferred_element_type=jnp.float32
        )
        row_delta = jnp.sum(softmax_w * grad_probs, -1, keepdims=True)
        grad_scores = (softmax_w * (grad_probs - row_delta)).astype(jnp.bfloat16)
        grad_query = (
            jnp.einsum(
                "hts,sd->htd", grad_scores, key_low[:row_stop], preferred_element_type=jnp.float32
            )
            * score_scale
        )
        grad_key = (
            jnp.einsum("hts,htd->sd", grad_scores, query_block, preferred_element_type=jnp.float32)
            * score_scale
        )
        fill = ((0, row_count - row_stop), (0, 0))
        return (jnp.pad(grad_key, fill), jnp.pad(grad_val, fill), grad_query)

    back_blocks = []
    for block_index in range(block_total):
        grad_key, grad_val, grad_query = back_block(block_index, query_low, grad_mixed)
        running = (down_sum, out_sum, gate_sum)
        grad_key, grad_val, grad_query, query_low, grad_mixed = tie(
            (grad_key, grad_val, grad_query, query_low, grad_mixed), running
        )
        back_blocks.append((grad_key, grad_val, grad_query))
    grad_keyrows = sum(block[0] for block in back_blocks)
    grad_values = sum(block[1] for block in back_blocks)
    grad_queries = jnp.concatenate([block[2] for block in back_blocks], 1)
    grad_query_raw, grad_query_gain = query_back(grad_queries)
    grad_query_raw = merge_heads(grad_query_raw.astype(jnp.bfloat16))
    grad_key_raw, grad_key_gain = key_back(grad_keyrows)
    grad_projected = jnp.concatenate(
        [grad_query_raw, grad_key_raw.astype(jnp.bfloat16), grad_values.astype(jnp.bfloat16)], -1
    )
    (grad_projected,) = tie((grad_projected,), (down_sum, out_sum))
    grad_inw = jnp.einsum(
        "td,tk->dk", normed_low, grad_projected, preferred_element_type=jnp.float32
    )
    grad_projected, grad_inw = tie(
        (grad_projected, grad_inw.astype(jnp.bfloat16)), (gate_sum,)
    )
    in_sum = Chain(matrix_steps(grad_inw, shards, groups, plain_bits))
    grad_normed = jnp.einsum(
        "tk,dk->td", grad_projected, in_full, preferred_element_type=jnp.float32
    )
    grad_stream_norm, grad_pre_attn = pre_attn_back(grad_normed)
    grad_input = (grad_resid + grad_stream_norm).astype(jnp.bfloat16)
    grad_gains = jnp.concatenate(
        [
            grad_pre_attn,
            grad_post_attn,
            grad_pre_ffn,
            grad_post_ffn,
            grad_query_gain,
            grad_key_gain,
        ],
        0,
    )
    gain_sum = Chain(gain_steps(grad_gains.reshape(shards, -1), shards, groups, plain_bits))
    tie((), (down_sum, out_sum, gate_sum, in_sum))
    running = (down_sum, out_sum, gate_sum, in_sum, gain_sum)
    while any(chain.result is None for chain in running):
        tie((), running)
    sum_down, sum_out, sum_gate, sum_in, sum_gains = (
        chain.finish().astype(jnp.float32) for chain in running
    )
    sum_gains = sum_gains.reshape(-1)
    new_in, in_momentum, in_variance = adamw(
        in_weight, sum_in, in_first, in_second, RATE_MATRIX, DECAY_MATRIX
    )
    new_out, out_momentum, out_variance = adamw(
        out_weight, sum_out, out_first, out_second, RATE_MATRIX, DECAY_MATRIX
    )
    new_gate, gate_momentum, gate_variance = adamw(
        gate_weight, sum_gate, gate_first, gate_second, RATE_MATRIX, DECAY_MATRIX
    )
    new_down, down_momentum, down_variance = adamw(
        down_weight, sum_down, down_first, down_second, RATE_MATRIX, DECAY_MATRIX
    )
    new_gains, gain_momentum, gain_variance = adamw(
        norm_gains, sum_gains, gain_first, gain_second, RATE_GAIN, 0.0
    )
    return (
        layer_out,
        grad_input,
        new_in,
        new_out,
        new_gate,
        new_down,
        new_gains,
        in_momentum,
        out_momentum,
        gate_momentum,
        down_momentum,
        gain_momentum,
        in_variance,
        out_variance,
        gate_variance,
        down_variance,
        gain_variance,
    )


def solution(mesh):
    in_specs = (
        P(("dp", "shard"), None),
        P(("dp", "shard"), None),
        P(("dp", "shard")),
        P("shard", None),
        P("shard", None),
        P("shard", None),
        P("shard", None),
        P("shard"),
        P("shard", None),
        P("shard", None),
        P("shard", None),
        P("shard", None),
        P("shard"),
        P("shard", None),
        P("shard", None),
        P("shard", None),
        P("shard", None),
        P("shard"),
    )
    out_specs = (
        P(("dp", "shard"), None),
        P(("dp", "shard"), None),
        P("shard", None),
        P("shard", None),
        P("shard", None),
        P("shard", None),
        P("shard"),
        P("shard", None),
        P("shard", None),
        P("shard", None),
        P("shard", None),
        P("shard"),
        P("shard", None),
        P("shard", None),
        P("shard", None),
        P("shard", None),
        P("shard"),
    )
    local = partial(body, groups=mesh.shape["dp"], shards=mesh.shape["shard"])
    return jax.shard_map(local, mesh=mesh, in_specs=in_specs, out_specs=out_specs, check_vma=False)
```
